32 devices in a mesh: spec: 8 (over y, x, core), wave: 4 (over z).
Axes of the slice: x: 2, y: 2, z: 4, core: 2. Of those that a mesh axis runs over, the one named last changes fastest.
Arguments:
- spectra: bfloat16 [8192, 7168], P('spec', 'wave'), may hold values from 0.049804688 to 5
- offsets: int32 [32], P('spec'), may hold values from 0 to 7167, as said below
- cover_lo: int32 [8192], P('spec'), may hold values from 0 to 7167, as said below
- cover_hi: int32 [8192], P('spec'), may hold values from 5377 to 7168
- coefficients: float32 [8192, 128], P('spec'), may hold values from 0.03 to 0.3
- templates: float32 [128, 7168], P(None, 'wave'), may hold values from 0.03 to 0.3
Outputs:
- templates_new: float32 [128, 7168], P(None, 'wave')
- coefficients_new: float32 [8192, 128], P('spec')
The draws below stay inside these ranges and needn't reach their ends.
Inputs may be any that keep to these rules, and one draw needn't show every extreme that they name: `offsets`: the first block of each index of spec has an offset of at least 5376; the last block's offset is 7167. cover_lo < cover_hi for every spectrum; about one spectrum in eight has weight one only on its last 1 to 4 observed pixels, cover_hi = 7168; the others have cover_lo < 1792 and cover_hi > 5376.
All inputs are finite; a program needn't handle non-finite values.
Results may differ from the reference program's by a relative error of at most 0.0012.
Values may be sent and summed in bfloat16 or wider, within the bound.
A program may use at most 128 MiB of HBM per device.

```python
import math
import jax
import jax.numpy as jnp
from jax import lax

PIX = 7168
RANK = 128
BLOCK = 256
SPEC_DEV = 1024
ITERS = 4
SPECTRA = 8192
BLOCKS = 32
N_SPEC = 8
N_WAVE = 4


def cover_pair(key):
    subkeys = jax.random.split(jax.random.fold_in(key, 7301), 4)
    wide_lo = jax.random.randint(subkeys[0], (SPECTRA,), 0, PIX // 4, dtype=jnp.int32)
    wide_hi = jax.random.randint(subkeys[1], (SPECTRA,), PIX - PIX // 4 + 1, PIX + 1, dtype=jnp.int32)
    narrow_len = jax.random.randint(subkeys[2], (SPECTRA,), 1, 5, dtype=jnp.int32)
    chosen = jax.random.randint(subkeys[3], (SPECTRA,), 0, 8, dtype=jnp.int32) == 0
    lower = jnp.where(chosen, PIX - narrow_len, wide_lo)
    upper = jnp.where(chosen, jnp.full((SPECTRA,), PIX, jnp.int32), wide_hi)
    return (lower, upper)


def draw_cover_lo(key, part):
    return cover_pair(key)[0]


def draw_cover_hi(key, part):
    return cover_pair(key)[1]


def draw_offsets(key, part):
    subkeys = jax.random.split(jax.random.fold_in(key, 5501), 2)
    spread = jax.random.randint(subkeys[0], (BLOCKS,), 0, PIX, dtype=jnp.int32)
    high = jax.random.randint(subkeys[1], (BLOCKS,), PIX - PIX // N_WAVE, PIX - PIX // (2 * N_WAVE), dtype=jnp.int32)
    index = jnp.arange(BLOCKS, dtype=jnp.int32)
    per_device = SPEC_DEV // BLOCK
    values = jnp.where(index % per_device == 0, high, spread)
    return jnp.where(index == BLOCKS - 1, jnp.full((BLOCKS,), PIX - 1, jnp.int32), values)


def steps_of(stream_key, dims, pieces, least, high):
    level, own = 1.0, jax.random.fold_in(stream_key, 6)
    for axis_at, parts in pieces:
        heights = jnp.exp(jax.random.uniform(jax.random.fold_in(own, axis_at), (parts,), jnp.float32, least / len(pieces), high / len(pieces)))
        level = level * jnp.repeat(heights, dims[axis_at] // parts).reshape([-1 if axis == axis_at else 1 for axis in range(len(dims))])
    return level


def setup_inputs(seed: int = 0) -> dict:
    keys = jax.random.split(jax.random.key(seed), 7)
    return {
        "spectra": jnp.clip(jnp.exp(math.log(5.0) - 4.609084 * jax.random.uniform(keys[0], (SPECTRA, PIX), jnp.float32) ** steps_of(keys[0], (SPECTRA, PIX), ((0, 8), (1, 4)), -0.2, 0.2)), 0.049804688, 5.0).astype(jnp.bfloat16),
        "offsets": draw_offsets(jax.random.fold_in(keys[6], 71), 0),
        "cover_lo": draw_cover_lo(jax.random.fold_in(keys[6], 71), 0),
        "cover_hi": draw_cover_hi(jax.random.fold_in(keys[6], 71), 0),
        "coefficients": jnp.clip(jnp.exp(math.log(0.3) - 2.3025852 * jax.random.uniform(keys[4], (SPECTRA, RANK), jnp.float32) ** steps_of(keys[4], (SPECTRA, RANK), ((0, 8),), -0.2, 0.2)), 0.03, 0.3),
        "templates": jnp.clip(jnp.exp(math.log(0.3) - 2.3025852 * jax.random.uniform(keys[5], (RANK, PIX), jnp.float32) ** steps_of(keys[5], (RANK, PIX), ((1, 4),), -0.2, 0.2)), 0.03, 0.3),
    }


def to_bf(value):
    return lax.optimization_barrier(value.astype(jnp.bfloat16)).astype(jnp.float32)


def matmul(left, right):
    return jnp.dot(left, right, precision=lax.Precision.HIGHEST)


def rest_span(fluxes, row_off, lo_rows, hi_rows):
    padded = jnp.concatenate([fluxes, jnp.zeros_like(fluxes)], axis=1)
    shifted = jax.vmap(lambda line, start: lax.dynamic_slice_in_dim(line, start, PIX, 0))(padded, row_off)
    pixel = jnp.arange(PIX, dtype=jnp.int32)
    observed = pixel[None, :] + row_off[:, None]
    inside = (observed >= lo_rows[:, None]) & (observed < hi_rows[:, None])
    return shifted.astype(jnp.float32), inside.astype(jnp.float32)


def ratio_of(rest, weight, model):
    return to_bf(jnp.where(weight > 0, rest / jnp.where(weight > 0, model, 1.0), 0.0))


def reference(spectra, offsets, cover_lo, cover_hi, coefficients, templates):
    row_off = jnp.repeat(offsets.astype(jnp.int32), BLOCK)
    flux_groups = spectra.reshape(N_SPEC, SPEC_DEV, PIX)
    off_groups = row_off.reshape(N_SPEC, SPEC_DEV)
    lo_groups = cover_lo.astype(jnp.int32).reshape(N_SPEC, SPEC_DEV)
    hi_groups = cover_hi.astype(jnp.int32).reshape(N_SPEC, SPEC_DEV)
    coef_groups = coefficients.reshape(N_SPEC, SPEC_DEV, RANK)
    temps = templates
    for update in range(ITERS):
        temps_bf = to_bf(temps)

        def stats(carry, item):
            fluxes, row_o, lo_rows, hi_rows, coef = item
            rest, weight = rest_span(fluxes, row_o, lo_rows, hi_rows)
            coef_bf = to_bf(coef)
            ratio = ratio_of(rest, weight, matmul(coef_bf, temps_bf))
            return (carry[0] + matmul(coef_bf.T, ratio), carry[1] + matmul(coef_bf.T, weight)), None

        start = jnp.zeros((RANK, PIX), jnp.float32)
        (num_t, den_t), unused = lax.scan(stats, (start, start), (flux_groups, off_groups, lo_groups, hi_groups, coef_groups))
        temps = temps * num_t / jnp.maximum(den_t, 1.0)
        temps_bf = to_bf(temps)

        def refresh(item):
            fluxes, row_o, lo_rows, hi_rows, coef = item
            rest, weight = rest_span(fluxes, row_o, lo_rows, hi_rows)
            coef_bf = to_bf(coef)
            ratio = ratio_of(rest, weight, matmul(coef_bf, temps_bf))
            num_c = matmul(ratio, temps_bf.T)
            den_c = matmul(weight, temps_bf.T)
            return coef * num_c / jnp.maximum(den_c, 1.0)

        coef_groups = lax.map(refresh, (flux_groups, off_groups, lo_groups, hi_groups, coef_groups))
    return temps, coef_groups.reshape(SPECTRA, RANK)
```

```python
import functools

import jax
import jax.numpy as jnp
from jax import lax
from jax.experimental import pallas as pl
from jax.experimental.pallas import tpu as pltpu
from jax.sharding import PartitionSpec as P

ITERS = 4
LANES = 128
MESH = pl.DeviceIdType.MESH
F32 = jnp.float32
BF16 = jnp.bfloat16


def shift_kernel(shift_ref, flux_ref, lo_ref, hi_ref, out_ref):
    shift = shift_ref[pl.program_id(0)]
    rows, width = flux_ref.shape
    lane = lax.broadcasted_iota(jnp.int32, (rows, LANES), 1)
    before = jnp.zeros((rows, LANES), F32)
    for tile in range(width // LANES + 1):
        if tile < width // LANES:
            now = flux_ref[:, tile * LANES : (tile + 1) * LANES].astype(F32)
            now = pltpu.roll(now, shift, 1)
        else:
            now = jnp.zeros((rows, LANES), F32)
        moved = jnp.where(lane < shift, before, now)
        column = lane + tile * LANES
        inside = (column >= lo_ref[...]) & (column < hi_ref[...])
        out_ref[:, tile * LANES : (tile + 1) * LANES] = jnp.where(inside, moved, 0.0).astype(BF16)
        before = now


def shifted_rest(spectra, shift, low, high, blocks):
    rows, width = spectra.shape
    per = rows // blocks
    return pl.pallas_call(
        shift_kernel,
        out_shape=jax.ShapeDtypeStruct((rows, width + LANES), BF16),
        grid_spec=pltpu.PrefetchScalarGridSpec(
            num_scalar_prefetch=1,
            grid=(blocks,),
            in_specs=[
                pl.BlockSpec((per, width), lambda i, s: (i, 0)),
                pl.BlockSpec((per, LANES), lambda i, s: (i, 0)),
                pl.BlockSpec((per, LANES), lambda i, s: (i, 0)),
            ],
            out_specs=pl.BlockSpec((per, width + LANES), lambda i, s: (i, 0)),
        ),
        compiler_params=pltpu.CompilerParams(vmem_limit_bytes=32 * 2**20),
    )(shift, spectra, low, high)


def main_kernel(
    n_spec,
    n_wave,
    first_ref,
    rest_ref,
    lo_ref,
    hi_ref,
    coef_ref,
    temp_ref,
    temps_out,
    coef_out,
    wbuf,
    wown,
    wfin,
    hb,
    hown,
    hfin,
    parts,
    send_a,
    recv_a,
    send_b,
    recv_b,
    send_z,
    recv_z,
    stat_c,
    recv_c,
    s_a,
    r_a,
    s_b,
    r_b,
    s_z,
    r_z,
    s_w,
    r_w,
    s_wb,
    r_wb,
    s_wc,
    r_wc,
    s_c,
    r_c,
    s_h,
    r_h,
    s_f,
    r_f,
    s_g,
    r_g,
):
    spec = lax.axis_index("spec")
    wave = lax.axis_index("wave")
    chips = n_spec // 2
    chip = spec // 2
    core = spec % 2
    buddy = 1 - core
    rows, _ = hb.shape
    blocks = first_ref.shape[0]
    per = rows // blocks
    own = rows // n_wave
    tiles = wbuf.shape[1]
    chunk = tiles // n_wave
    rank_part = wbuf.shape[2]
    rank = n_spec * rank_part
    spans = rest_ref.shape[1] // LANES
    group = max(g for g in range(1, 6) if spans % g == 0)
    own_rows = pl.ds(pl.multiple_of(wave * own, own), own)

    def to_chip(k):
        return (lax.rem(chip + k, chips) * 2 + core, wave)

    def to_buddy():
        return (chip * 2 + buddy, wave)

    def to_wave(k):
        return (spec, lax.rem(wave + k, n_wave))

    def to_spec(k):
        return (lax.rem(spec + k, n_spec), wave)

    def copy(src, dst, send, recv, device):
        return pltpu.make_async_remote_copy(
            src_ref=src, dst_ref=dst, send_sem=send, recv_sem=recv, device_id=device, device_id_type=MESH
        )

    def part_of(k):
        return pl.ds(lax.rem(wave + k, n_wave) * chunk, chunk)

    def part_from(k):
        return pl.ds(lax.rem(wave + n_wave - k, n_wave) * chunk, chunk)

    barrier = pltpu.get_barrier_semaphore()
    for k in range(1, n_spec):
        pl.semaphore_signal(barrier, inc=1, device_id=to_spec(k), device_id_type=MESH)
    for k in range(1, n_wave):
        pl.semaphore_signal(barrier, inc=1, device_id=to_wave(k), device_id_type=MESH)
    pl.semaphore_wait(barrier, n_spec + n_wave - 2)

    def gather_templates():
        over_z = [None] + [
            copy(wbuf.at[spec, part_of(0)], wbuf.at[spec, part_of(0)], s_w.at[k], r_w.at[k], to_wave(k))
            for k in range(1, n_wave)
        ]
        over_chips = {}
        over_core = {}
        for kz in range(n_wave):
            for k in range(chips):
                slot = wbuf.at[lax.rem(chip + chips - k, chips) * 2 + core, part_from(kz)]
                over_core[kz, k] = copy(slot, slot, s_wc.at[kz, k], r_wc.at[kz, k], to_buddy())
                if k:
                    mine = wbuf.at[spec, part_from(kz)]
                    over_chips[kz, k] = copy(mine, mine, s_wb.at[kz, k], r_wb.at[kz, k], to_chip(k))
        for k in range(1, n_wave):
            over_z[k].start()
        for kz in range(n_wave):
            if kz:
                over_z[kz].wait_recv()
            for k in range(1, chips):
                over_chips[kz, k].start()
            over_core[kz, 0].start()
        for kz in range(n_wave):
            for k in range(1, chips):
                over_chips[kz, k].wait_recv()
                over_core[kz, k].start()
        for kz in range(n_wave):
            for k in range(chips):
                over_core[kz, k].wait()
                if k:
                    over_chips[kz, k].wait_send()
            if kz:
                over_z[kz].wait_send()

    def tile_of(index):
        piece = wbuf[:, index]
        if rank_part % 16:
            return piece.astype(F32).reshape(rank, LANES).astype(BF16)
        return piece.reshape(rank, LANES)

    def ratio_of(block, g):
        at = pl.ds(pl.multiple_of(block * per, per), per)
        start = first_ref[block] + g * group
        temps = jnp.concatenate(
            [tile_of(jnp.clip(start + k, 0, tiles - 1)) for k in range(group)], axis=1
        )
        model = jnp.dot(hb[at, :], temps, preferred_element_type=F32)
        rest = rest_ref[at, g * group * LANES : (g + 1) * group * LANES].astype(F32)
        return temps, jnp.where(rest > 0, rest / model, 0.0).astype(BF16)

    def put_stat(index, value):
        for part in range(n_spec):
            send_a[part % 2, part // 2, index] = value[part * rank_part : (part + 1) * rank_part]

    def mask_of(low, high, first):
        pixel = lax.broadcasted_iota(jnp.int32, low.shape, 1) + first
        return jnp.where((pixel >= low) & (pixel < high), 1.0, 0.0).astype(BF16)

    wown[...] = temp_ref[...]
    wbuf[spec, part_of(0)] = temp_ref[...].astype(BF16)
    hb[...] = coef_ref[...].astype(BF16)
    hown[...] = coef_ref[own_rows, :]
    for block in range(blocks):
        parts[block, 0] = jnp.zeros((rank, LANES), F32)
        parts[block, spans + 1] = jnp.zeros((rank, LANES), F32)
    gather_templates()

    last_temps = [
        copy(wown, wfin.at[spec], s_f.at[k], r_f.at[k], to_spec(k)) for k in range(1, n_spec)
    ]
    order = list(range(1, n_wave)) + [0]

    def update(step, unused):
        def block_stats(block, unused):
            at = pl.ds(pl.multiple_of(block * per, per), per)
            for g in range(spans // group):
                temps, ratio = ratio_of(block, g)
                num = lax.dot_general(
                    hb[at, :], ratio, (((0,), (0,)), ((), ())), preferred_element_type=F32
                )
                for k in range(group):
                    parts[block, 1 + g * group + k] = num[:, k * LANES : (k + 1) * LANES]
            return 0

        lax.fori_loop(0, blocks, block_stats, 0)

        copies_a = {}
        copies_b = {}
        for kz in range(n_wave + 1):
            where = part_of(kz) if kz < n_wave else pl.ds(tiles, chunk)
            copies_a[kz] = copy(
                send_a.at[buddy, :, where], recv_a.at[:, where], s_a.at[kz], r_a.at[kz], to_buddy()
            )
            for k in range(1, chips):
                copies_b[kz, k] = copy(
                    send_b.at[lax.rem(chip + k, chips), where],
                    recv_b.at[k - 1, where],
                    s_b.at[kz, k],
                    r_b.at[kz, k],
                    to_chip(k),
                )
        copies_z = {
            k: copy(send_z.at[part_of(k)], recv_z.at[k - 1], s_z.at[k], r_z.at[k], to_wave(k))
            for k in range(1, n_wave)
        }

        for kz in order:
            first = lax.rem(wave + kz, n_wave) * chunk

            def add_blocks(i, unused):
                index = first + i
                total = parts[0, jnp.clip(index - first_ref[0], -1, spans) + 1]
                for block in range(1, blocks):
                    total = total + parts[block, jnp.clip(index - first_ref[block], -1, spans) + 1]
                put_stat(index, total)
                return 0

            lax.fori_loop(0, chunk, add_blocks, 0)
            copies_a[kz].start()

        def den_tile(i, unused):
            mask = mask_of(lo_ref[...], hi_ref[...], (wave * chunk + i) * LANES)
            put_stat(
                tiles + i,
                lax.dot_general(hb[...], mask, (((0,), (0,)), ((), ())), preferred_element_type=F32),
            )
            return 0

        lax.fori_loop(0, chunk, den_tile, 0)
        copies_a[n_wave].start()

        for kz in order + [n_wave]:
            first = lax.rem(wave + kz, n_wave) * chunk if kz < n_wave else tiles
            copies_a[kz].wait_recv()

            def add_core(i, unused):
                for c in range(chips):
                    send_b[c, first + i] = (
                        send_a[core, c, first + i] + recv_a[c, first + i]
                    ).astype(send_b.dtype)
                return 0

            lax.fori_loop(0, chunk, add_core, 0)
            for k in range(1, chips):
                copies_b[kz, k].start()

        def chip_sum(index):
            total = send_a[core, chip, index] + recv_a[chip, index]
            for k in range(1, chips):
                total = total + recv_b[k - 1, index].astype(F32)
            return total

        for kz in order[:-1]:
            first = lax.rem(wave + kz, n_wave) * chunk
            for k in range(1, chips):
                copies_b[kz, k].wait_recv()

            def add_chips(i, unused):
                send_z[first + i] = chip_sum(first + i)
                return 0

            lax.fori_loop(0, chunk, add_chips, 0)
            copies_z[kz].start()
        for kz in (0, n_wave):
            for k in range(1, chips):
                copies_b[kz, k].wait_recv()
        for k in range(1, n_wave):
            copies_z[k].wait_recv()

        def new_tile(i, unused):
            num = chip_sum(wave * chunk + i)
            for k in range(1, n_wave):
                num = num + recv_z[k - 1, i]
            value = wown[i] * num / jnp.maximum(chip_sum(tiles + i), 1.0)
            wown[i] = value
            wbuf[spec, wave * chunk + i] = value.astype(BF16)
            return 0

        lax.fori_loop(0, chunk, new_tile, 0)
        for kz in range(n_wave + 1):
            copies_a[kz].wait_send()
            for k in range(1, chips):
                copies_b[kz, k].wait_send()
        for k in range(1, n_wave):
            copies_z[k].wait_send()

        gather_templates()

        @pl.when(step == ITERS - 1)
        def _():
            for one in last_temps:
                one.start()

        def block_coefs(block, unused):
            at = pl.ds(pl.multiple_of(block * per, per), per)
            total = jnp.zeros((per, rank), F32)
            for g in range(spans // group):
                temps, ratio = ratio_of(block, g)
                total = total + lax.dot_general(
                    ratio, temps, (((1,), (1,)), ((), ())), preferred_element_type=F32
                )
            stat_c[at, :] = total
            return 0

        lax.fori_loop(0, blocks, block_coefs, 0)
        copies_c = []
        for k in range(1, n_wave):
            theirs = pl.ds(pl.multiple_of(lax.rem(wave + k, n_wave) * own, own), own)
            copies_c.append(
                copy(stat_c.at[theirs], recv_c.at[k - 1], s_c.at[k], r_c.at[k], to_wave(k))
            )
        for one in copies_c:
            one.start()

        def den_coef(i, total):
            masks = []
            temps = []
            for k in range(4):
                masks.append(mask_of(lo_ref[own_rows, :], hi_ref[own_rows, :], (i * 4 + k) * LANES))
                temps.append(tile_of(i * 4 + k))
            return total + lax.dot_general(
                jnp.concatenate(masks, axis=1),
                jnp.concatenate(temps, axis=1),
                (((1,), (1,)), ((), ())),
                preferred_element_type=F32,
            )

        den = lax.fori_loop(0, tiles // 4, den_coef, jnp.zeros((own, rank), F32))
        for one in copies_c:
            one.wait_recv()
        num = stat_c[own_rows, :]
        for k in range(1, n_wave):
            num = num + recv_c[k - 1]
        value = hown[...] * num / jnp.maximum(den, 1.0)
        hown[...] = value
        for one in copies_c:
            one.wait_send()

        @pl.when(step < ITERS - 1)
        def _():
            hb[own_rows, :] = value.astype(BF16)
            copies_h = [
                copy(hb.at[own_rows], hb.at[own_rows], s_h.at[k], r_h.at[k], to_wave(k))
                for k in range(1, n_wave)
            ]
            for one in copies_h:
                one.start()
            for one in copies_h:
                one.wait()

        return 0

    lax.fori_loop(0, ITERS, update, 0)

    last_coefs = [
        copy(hown, hfin.at[wave], s_g.at[k], r_g.at[k], to_wave(k)) for k in range(1, n_wave)
    ]
    for one in last_coefs:
        one.start()
    wfin[spec] = wown[...]
    hfin[wave] = hown[...]
    for one in last_temps:
        one.wait()
    for i in range(chunk):
        temps_out[:, i * LANES : (i + 1) * LANES] = wfin[:, i].reshape(rank, LANES)
    for one in last_coefs:
        one.wait()
    for k in range(n_wave):
        coef_out[k * own : (k + 1) * own, :] = hfin[k]


def shards(n_spec, n_wave, spectra, offsets, cover_lo, cover_hi, coefficients, templates):
    rows, width = spectra.shape
    rank = templates.shape[0]
    blocks = offsets.shape[0]
    chips = n_spec // 2
    chunk = width // LANES
    tiles = chunk * n_wave
    part = rank // n_spec
    own = rows // n_wave
    wave = lax.axis_index("wave")
    spec = lax.axis_index("spec")

    base = wave * width - offsets
    shift = jnp.mod(base, LANES)
    first = (base - shift) // LANES
    row_off, row_shift = (jnp.repeat(v, rows // blocks) for v in (offsets, shift))
    begin = wave * width
    low = jnp.maximum(jnp.maximum(cover_lo - begin, 0), row_off - begin) + row_shift
    high = jnp.minimum(cover_hi - begin, width) + row_shift

    def spread(value):
        return jnp.broadcast_to(value[:, None], (rows, LANES))

    rest = shifted_rest(spectra, shift, spread(low), spread(high), blocks)
    mine = lax.dynamic_slice_in_dim(templates, spec * part, part, 0)
    mine = mine.reshape(part, chunk, LANES).transpose(1, 0, 2)

    vmem = pl.BlockSpec(memory_space=pltpu.VMEM)
    dma = pltpu.SemaphoreType.DMA
    return pl.pallas_call(
        functools.partial(main_kernel, n_spec, n_wave),
        out_shape=(
            jax.ShapeDtypeStruct((rank, width), F32),
            jax.ShapeDtypeStruct((rows, rank), F32),
        ),
        in_specs=[pl.BlockSpec(memory_space=pltpu.SMEM)] + [vmem] * 5,
        out_specs=(vmem, vmem),
        scratch_shapes=[
            pltpu.VMEM((n_spec, tiles, part, LANES), BF16),
            pltpu.VMEM((chunk, part, LANES), F32),
            pltpu.VMEM((n_spec, chunk, part, LANES), F32),
            pltpu.VMEM((rows, rank), BF16),
            pltpu.VMEM((own, rank), F32),
            pltpu.VMEM((n_wave, own, rank), F32),
            pltpu.VMEM((blocks, chunk + 3, rank, LANES), F32),
            pltpu.VMEM((2, chips, tiles + chunk, part, LANES), F32),
            pltpu.VMEM((chips, tiles + chunk, part, LANES), F32),
            pltpu.VMEM((chips, tiles + chunk, part, LANES), F32),
            pltpu.VMEM((chips - 1, tiles + chunk, part, LANES), F32),
            pltpu.VMEM((tiles, part, LANES), F32),
            pltpu.VMEM((n_wave - 1, chunk, part, LANES), F32),
            pltpu.VMEM((rows, rank), F32),
            pltpu.VMEM((n_wave - 1, own, rank), F32),
        ]
        + [dma((n_wave + 1,))] * 2
        + [dma((n_wave + 1, chips))] * 2
        + [dma((n_wave,))] * 2
        + [dma((n_wave,))] * 2
        + [dma((n_wave, chips))] * 4
        + [dma((n_wave,))] * 2
        + [dma((n_wave,))] * 2
        + [dma((n_spec,))] * 2
        + [dma((n_wave,))] * 2,
        compiler_params=pltpu.CompilerParams(
            collective_id=0, has_side_effects=True, vmem_limit_bytes=48 * 2**20
        ),
    )(
        first,
        rest,
        spread(cover_lo - row_off),
        spread(cover_hi - row_off),
        coefficients,
        mine,
    )


def solution(mesh):
    in_specs = (
        P("spec", "wave"),
        P("spec"),
        P("spec"),
        P("spec"),
        P("spec", None),
        P(None, "wave"),
    )
    out_specs = (P(None, "wave"), P("spec", None))
    return jax.shard_map(
        functools.partial(shards, mesh.shape["spec"], mesh.shape["wave"]),
        mesh=mesh,
        in_specs=in_specs,
        out_specs=out_specs,
        check_vma=False,
    )
```

```python
import functools

import jax
import jax.numpy as jnp
from jax import lax
from jax.experimental import pallas as pl
from jax.experimental.pallas import tpu as pltpu
from jax.sharding import PartitionSpec as P

ITERS = 4
LANES = 128
MESH = pl.DeviceIdType.MESH
F32 = jnp.float32
BF16 = jnp.bfloat16


def shift_kernel(shift_ref, flux_ref, lo_ref, hi_ref, out_ref):
    shift = shift_ref[pl.program_id(0)]
    rows, width = flux_ref.shape
    lane = lax.broadcasted_iota(jnp.int32, (rows, LANES), 1)
    before = jnp.zeros((rows, LANES), F32)
    for tile in range(width // LANES + 1):
        if tile < width // LANES:
            now = flux_ref[:, tile * LANES : (tile + 1) * LANES].astype(F32)
            now = pltpu.roll(now, shift, 1)
        else:
            now = jnp.zeros((rows, LANES), F32)
        moved = jnp.where(lane < shift, before, now)
        column = lane + tile * LANES
        inside = (column >= lo_ref[...]) & (column < hi_ref[...])
        out_ref[:, tile * LANES : (tile + 1) * LANES] = jnp.where(inside, moved, 0.0).astype(BF16)
        before = now


def shifted_rest(spectra, shift, low, high, blocks):
    rows, width = spectra.shape
    per = rows // blocks
    return pl.pallas_call(
        shift_kernel,
        out_shape=jax.ShapeDtypeStruct((rows, width + LANES), BF16),
        grid_spec=pltpu.PrefetchScalarGridSpec(
            num_scalar_prefetch=1,
            grid=(blocks,),
            in_specs=[
                pl.BlockSpec((per, width), lambda i, s: (i, 0)),
                pl.BlockSpec((per, LANES), lambda i, s: (i, 0)),
                pl.BlockSpec((per, LANES), lambda i, s: (i, 0)),
            ],
            out_specs=pl.BlockSpec((per, width + LANES), lambda i, s: (i, 0)),
        ),
        compiler_params=pltpu.CompilerParams(vmem_limit_bytes=32 * 2**20),
    )(shift, spectra, low, high)


def main_kernel(
    n_spec,
    n_wave,
    first_ref,
    rest_ref,
    lo_ref,
    hi_ref,
    coef_ref,
    temp_ref,
    temps_out,
    coef_out,
    wbuf,
    wown,
    wfin,
    hb,
    hown,
    hfin,
    parts,
    send_a,
    recv_a,
    send_b,
    recv_b,
    wide_b,
    recv_wb,
    keep_b,
    send_z,
    recv_z,
    send_c,
    recv_c,
    wide_c,
    recv_wc,
    keep_c,
    den_c,
    s_a,
    r_a,
    s_b,
    r_b,
    s_z,
    r_z,
    s_w,
    r_w,
    s_wb,
    r_wb,
    s_wc,
    r_wc,
    s_c,
    r_c,
    s_h,
    r_h,
    s_f,
    r_f,
    s_g,
    r_g,
):
    spec = lax.axis_index("spec")
    wave = lax.axis_index("wave")
    chips = n_spec // 2
    chip = spec // 2
    core = spec % 2
    buddy = 1 - core
    rows, _ = hb.shape
    blocks = first_ref.shape[0]
    per = rows // blocks
    own = rows // n_wave
    tiles = wbuf.shape[1]
    chunk = tiles // n_wave
    rank_part = wbuf.shape[2]
    rank = n_spec * rank_part
    spans = rest_ref.shape[1] // LANES
    group = max(g for g in range(1, 6) if spans % g == 0)
    some = max(g for g in range(1, 8) if chunk % g == 0)
    unit = min(own, per)
    units = rows // unit
    own_rows = pl.ds(pl.multiple_of(wave * own, own), own)

    def to_chip(k):
        return (lax.rem(chip + k, chips) * 2 + core, wave)

    def to_buddy():
        return (chip * 2 + buddy, wave)

    def to_wave(k):
        return (spec, lax.rem(wave + k, n_wave))

    def to_spec(k):
        return (lax.rem(spec + k, n_spec), wave)

    def copy(src, dst, send, recv, device):
        return pltpu.make_async_remote_copy(
            src_ref=src, dst_ref=dst, send_sem=send, recv_sem=recv, device_id=device, device_id_type=MESH
        )

    def part_of(k):
        return pl.ds(lax.rem(wave + k, n_wave) * chunk, chunk)

    def part_from(k):
        return pl.ds(lax.rem(wave + n_wave - k, n_wave) * chunk, chunk)

    barrier = pltpu.get_barrier_semaphore()
    for k in range(1, n_spec):
        pl.semaphore_signal(barrier, inc=1, device_id=to_spec(k), device_id_type=MESH)
    for k in range(1, n_wave):
        pl.semaphore_signal(barrier, inc=1, device_id=to_wave(k), device_id_type=MESH)
    pl.semaphore_wait(barrier, n_spec + n_wave - 2)

    def gather_templates(arrived=None):
        over_z = [None] + [
            copy(wbuf.at[spec, part_of(0)], wbuf.at[spec, part_of(0)], s_w.at[k], r_w.at[k], to_wave(k))
            for k in range(1, n_wave)
        ]
        over_chips = {}
        over_core = {}
        for kz in range(n_wave):
            for k in range(chips):
                slot = wbuf.at[lax.rem(chip + chips - k, chips) * 2 + core, part_from(kz)]
                over_core[kz, k] = copy(slot, slot, s_wc.at[kz, k], r_wc.at[kz, k], to_buddy())
                if k:
                    mine = wbuf.at[spec, part_from(kz)]
                    over_chips[kz, k] = copy(mine, mine, s_wb.at[kz, k], r_wb.at[kz, k], to_chip(k))
        for k in range(1, n_wave):
            over_z[k].start()
        for kz in range(n_wave):
            if kz:
                over_z[kz].wait_recv()
            for k in range(1, chips):
                over_chips[kz, k].start()
            over_core[kz, 0].start()
        for kz in range(n_wave + 1):
            if kz < n_wave:
                for k in range(1, chips):
                    over_chips[kz, k].wait_recv()
                    over_core[kz, k].start()
            if kz:
                for k in range(chips):
                    over_core[kz - 1, k].wait_recv()
                if arrived is not None:
                    arrived(kz - 1)
        for kz in range(n_wave):
            for k in range(chips):
                over_core[kz, k].wait_send()
                if k:
                    over_chips[kz, k].wait_send()
            if kz:
                over_z[kz].wait_send()

    def tile_of(index):
        piece = wbuf[:, index]
        if rank_part % 16:
            return piece.astype(F32).reshape(rank, LANES).astype(BF16)
        return piece.reshape(rank, LANES)

    def rows_of(at):
        return pl.ds(pl.multiple_of(at * unit, unit), unit)

    def ratio_of(at, g):
        start = first_ref[at * unit // per] + g * group
        temps = jnp.concatenate(
            [tile_of(jnp.clip(start + k, 0, tiles - 1)) for k in range(group)], axis=1
        )
        model = jnp.dot(hb[rows_of(at), :], temps, preferred_element_type=F32)
        rest = rest_ref[rows_of(at), g * group * LANES : (g + 1) * group * LANES].astype(F32)
        return temps, jnp.where(rest > 0, rest / model, 0.0).astype(BF16)

    def rounded(value, share):
        wanted = value * share
        sent = wanted.astype(BF16)
        back = sent.astype(F32)
        left = jnp.where(back > 0, wanted / back, 1.0)
        return sent, jnp.clip(left, 0.99, 1.01)

    def put_stat(index, value):
        for part in range(n_spec):
            send_a[part % 2, part // 2, index] = value[part * rank_part : (part + 1) * rank_part]

    def mask_of(low, high, first):
        pixel = lax.broadcasted_iota(jnp.int32, low.shape, 1) + first
        return jnp.where((pixel >= low) & (pixel < high), 1.0, 0.0).astype(BF16)

    def coef_copies():
        return [
            copy(hb.at[own_rows], hb.at[own_rows], s_h.at[k], r_h.at[k], to_wave(k))
            for k in range(1, n_wave)
        ]

    wown[...] = temp_ref[...]
    wbuf[spec, part_of(0)] = temp_ref[...].astype(BF16)
    hb[own_rows, :] = coef_ref[own_rows, :].astype(BF16)
    hown[...] = coef_ref[own_rows, :]
    for one in coef_copies():
        one.start()
    for at in range(units):
        parts[at, 0] = jnp.zeros((rank, LANES), F32)
        parts[at, spans + 1] = jnp.zeros((rank, LANES), F32)
    keep_b[...] = jnp.ones_like(keep_b)
    keep_c[...] = jnp.ones_like(keep_c)
    gather_templates()

    last_temps = [
        copy(wown, wfin.at[spec], s_f.at[k], r_f.at[k], to_spec(k)) for k in range(1, n_spec)
    ]
    order = list(range(1, n_wave)) + [0]

    def update(last):
        out_b, in_b = (wide_b, recv_wb) if last else (send_b, recv_b)
        out_c, in_c = (wide_c, recv_wc) if last else (send_c, recv_c)

        copies_h = coef_copies()
        for kz in range(n_wave):
            if kz:
                copies_h[kz - 1].wait()
            for j in range(own // unit):
                at = lax.rem(wave + n_wave - kz, n_wave) * (own // unit) + j
                for g in range(spans // group):
                    temps, ratio = ratio_of(at, g)
                    num = lax.dot_general(
                        hb[rows_of(at), :], ratio, (((0,), (0,)), ((), ())), preferred_element_type=F32
                    )
                    for k in range(group):
                        parts[at, 1 + g * group + k] = num[:, k * LANES : (k + 1) * LANES]

        copies_a = {}
        copies_b = {}
        for kz in range(n_wave + 1):
            where = part_of(kz) if kz < n_wave else pl.ds(tiles, chunk)
            copies_a[kz] = copy(
                send_a.at[buddy, :, where], recv_a.at[:, where], s_a.at[kz], r_a.at[kz], to_buddy()
            )
            for k in range(1, chips):
                source, target = (out_b, in_b) if kz < n_wave else (wide_b, recv_wb)
                copies_b[kz, k] = copy(
                    source.at[k - 1, where], target.at[k - 1, where], s_b.at[kz, k], r_b.at[kz, k], to_chip(k)
                )
        copies_z = {
            k: copy(send_z.at[k - 1], recv_z.at[k - 1], s_z.at[k], r_z.at[k], to_wave(k))
            for k in range(1, n_wave)
        }

        for kz in order:
            first = lax.rem(wave + kz, n_wave) * chunk

            def add_blocks(i, unused):
                index = first + i
                total = None
                for at in range(units):
                    place = jnp.clip(index - first_ref[at * unit // per], -1, spans) + 1
                    total = parts[at, place] if at == 0 else total + parts[at, place]
                put_stat(index, total)
                return 0

            lax.fori_loop(0, chunk, add_blocks, 0)
            copies_a[kz].start()

        def den_tile(i, unused):
            mask = mask_of(lo_ref[...], hi_ref[...], (wave * chunk + i) * LANES)
            put_stat(
                tiles + i,
                lax.dot_general(hb[...], mask, (((0,), (0,)), ((), ())), preferred_element_type=F32),
            )
            return 0

        lax.fori_loop(0, chunk, den_tile, 0)
        copies_a[n_wave].start()

        for kz in order + [n_wave]:
            first = lax.rem(wave + kz, n_wave) * chunk if kz < n_wave else tiles
            copies_a[kz].wait_recv()

            def add_core(i, unused):
                index = first + i
                for k in range(1, chips):
                    c = lax.rem(chip + k, chips)
                    value = send_a[core, c, index] + recv_a[c, index]
                    if kz == n_wave:
                        wide_b[k - 1, index] = value
                    elif last:
                        out_b[k - 1, index] = value * keep_b[k - 1, index]
                    else:
                        out_b[k - 1, index], keep_b[k - 1, index] = rounded(value, keep_b[k - 1, index])
                return 0

            lax.fori_loop(0, chunk, add_core, 0)
            for k in range(1, chips):
                copies_b[kz, k].start()

        def chip_sum(index, landed=in_b):
            total = send_a[core, chip, index] + recv_a[chip, index]
            for k in range(1, chips):
                total = total + landed[k - 1, index].astype(F32)
            return total

        for kz in order[:-1]:
            first = lax.rem(wave + kz, n_wave) * chunk
            for k in range(1, chips):
                copies_b[kz, k].wait_recv()

            def add_chips(i, unused):
                send_z[kz - 1, i] = chip_sum(first + i)
                return 0

            lax.fori_loop(0, chunk, add_chips, 0)
            copies_z[kz].start()
        for kz in (0, n_wave):
            for k in range(1, chips):
                copies_b[kz, k].wait_recv()
        for k in range(1, n_wave):
            copies_z[k].wait_recv()

        def new_tile(i, unused):
            num = chip_sum(wave * chunk + i)
            for k in range(1, n_wave):
                num = num + recv_z[k - 1, i]
            value = wown[i] * num / jnp.maximum(chip_sum(tiles + i, recv_wb), 1.0)
            wown[i] = value
            wbuf[spec, wave * chunk + i] = value.astype(BF16)
            return 0

        lax.fori_loop(0, chunk, new_tile, 0)
        for kz in range(n_wave + 1):
            copies_a[kz].wait_send()
            for k in range(1, chips):
                copies_b[kz, k].wait_send()
        for k in range(1, n_wave):
            copies_z[k].wait_send()

        den_c[...] = jnp.zeros_like(den_c)

        def add_den(kz):
            first = lax.rem(wave + n_wave - kz, n_wave) * chunk

            def some_tiles(i, unused):
                index = first + i * some
                masks = [
                    mask_of(lo_ref[own_rows, :], hi_ref[own_rows, :], (index + k) * LANES)
                    for k in range(some)
                ]
                den_c[...] += lax.dot_general(
                    jnp.concatenate(masks, axis=1),
                    jnp.concatenate([tile_of(index + k) for k in range(some)], axis=1),
                    (((1,), (1,)), ((), ())),
                    preferred_element_type=F32,
                )
                return 0

            lax.fori_loop(0, chunk // some, some_tiles, 0)

        gather_templates(add_den)

        if last:
            for one in last_temps:
                one.start()

        copies_c = [
            copy(out_c.at[k - 1], in_c.at[k - 1], s_c.at[k], r_c.at[k], to_wave(k))
            for k in range(1, n_wave)
        ]
        mine = None
        for kz in order:
            pieces = []
            for j in range(own // unit):
                at = lax.rem(wave + kz, n_wave) * (own // unit) + j
                total = None
                for g in range(spans // group):
                    temps, ratio = ratio_of(at, g)
                    num = lax.dot_general(
                        ratio, temps, (((1,), (1,)), ((), ())), preferred_element_type=F32
                    )
                    total = num if g == 0 else total + num
                pieces.append(total)
            total = pieces[0] if len(pieces) == 1 else jnp.concatenate(pieces, axis=0)
            if kz == 0:
                mine = total
            else:
                if last:
                    out_c[kz - 1] = total * keep_c[kz - 1]
                else:
                    out_c[kz - 1], keep_c[kz - 1] = rounded(total, keep_c[kz - 1])
                copies_c[kz - 1].start()
        for one in copies_c:
            one.wait_recv()
        for k in range(1, n_wave):
            mine = mine + in_c[k - 1].astype(F32)
        value = hown[...] * mine / jnp.maximum(den_c[...], 1.0)
        hown[...] = value
        for one in copies_c:
            one.wait_send()
        if not last:
            hb[own_rows, :] = value.astype(BF16)
            for one in coef_copies():
                one.start()

    def step(i, unused):
        update(False)
        return 0

    lax.fori_loop(0, ITERS - 1, step, 0)
    update(True)

    last_coefs = [
        copy(hown, hfin.at[wave], s_g.at[k], r_g.at[k], to_wave(k)) for k in range(1, n_wave)
    ]
    for one in last_coefs:
        one.start()
    wfin[spec] = wown[...]
    hfin[wave] = hown[...]
    for one in last_temps:
        one.wait()
    for i in range(chunk):
        temps_out[:, i * LANES : (i + 1) * LANES] = wfin[:, i].reshape(rank, LANES)
    for one in last_coefs:
        one.wait()
    for k in range(n_wave):
        coef_out[k * own : (k + 1) * own, :] = hfin[k]


def shards(n_spec, n_wave, spectra, offsets, cover_lo, cover_hi, coefficients, templates):
    rows, width = spectra.shape
    rank = templates.shape[0]
    blocks = offsets.shape[0]
    chips = n_spec // 2
    chunk = width // LANES
    tiles = chunk * n_wave
    part = rank // n_spec
    own = rows // n_wave
    wave = lax.axis_index("wave")
    spec = lax.axis_index("spec")

    base = wave * width - offsets
    shift = jnp.mod(base, LANES)
    first = (base - shift) // LANES
    row_off, row_shift = (jnp.repeat(v, rows // blocks) for v in (offsets, shift))
    begin = wave * width
    low = jnp.maximum(jnp.maximum(cover_lo - begin, 0), row_off - begin) + row_shift
    high = jnp.minimum(cover_hi - begin, width) + row_shift

    def spread(value):
        return jnp.broadcast_to(value[:, None], (rows, LANES))

    rest = shifted_rest(spectra, shift, spread(low), spread(high), blocks)
    mine = lax.dynamic_slice_in_dim(templates, spec * part, part, 0)
    mine = mine.reshape(part, chunk, LANES).transpose(1, 0, 2)

    vmem = pl.BlockSpec(memory_space=pltpu.VMEM)
    dma = pltpu.SemaphoreType.DMA
    return pl.pallas_call(
        functools.partial(main_kernel, n_spec, n_wave),
        out_shape=(
            jax.ShapeDtypeStruct((rank, width), F32),
            jax.ShapeDtypeStruct((rows, rank), F32),
        ),
        in_specs=[pl.BlockSpec(memory_space=pltpu.SMEM)] + [vmem] * 5,
        out_specs=(vmem, vmem),
        scratch_shapes=[
            pltpu.VMEM((n_spec, tiles, part, LANES), BF16),
            pltpu.VMEM((chunk, part, LANES), F32),
            pltpu.VMEM((n_spec, chunk, part, LANES), F32),
            pltpu.VMEM((rows, rank), BF16),
            pltpu.VMEM((own, rank), F32),
            pltpu.VMEM((n_wave, own, rank), F32),
            pltpu.VMEM((rows // min(own, rows // blocks), chunk + 3, rank, LANES), F32),
            pltpu.VMEM((2, chips, tiles + chunk, part, LANES), F32),
            pltpu.VMEM((chips, tiles + chunk, part, LANES), F32),
            pltpu.VMEM((chips - 1, tiles + chunk, part, LANES), BF16),
            pltpu.VMEM((chips - 1, tiles + chunk, part, LANES), BF16),
            pltpu.VMEM((chips - 1, tiles + chunk, part, LANES), F32),
            pltpu.VMEM((chips - 1, tiles + chunk, part, LANES), F32),
            pltpu.VMEM((chips - 1, tiles + chunk, part, LANES), F32),
            pltpu.VMEM((n_wave - 1, chunk, part, LANES), F32),
            pltpu.VMEM((n_wave - 1, chunk, part, LANES), F32),
            pltpu.VMEM((n_wave - 1, own, rank), BF16),
            pltpu.VMEM((n_wave - 1, own, rank), BF16),
            pltpu.VMEM((n_wave - 1, own, rank), F32),
            pltpu.VMEM((n_wave - 1, own, rank), F32),
            pltpu.VMEM((n_wave - 1, own, rank), F32),
            pltpu.VMEM((own, rank), F32),
        ]
        + [dma((n_wave + 1,))] * 2
        + [dma((n_wave + 1, chips))] * 2
        + [dma((n_wave,))] * 2
        + [dma((n_wave,))] * 2
        + [dma((n_wave, chips))] * 4
        + [dma((n_wave,))] * 2
        + [dma((n_wave,))] * 2
        + [dma((n_spec,))] * 2
        + [dma((n_wave,))] * 2,
        compiler_params=pltpu.CompilerParams(
            collective_id=0, has_side_effects=True, vmem_limit_bytes=48 * 2**20
        ),
    )(
        first,
        rest,
        spread(cover_lo - row_off),
        spread(cover_hi - row_off),
        coefficients,
        mine,
    )


def solution(mesh):
    in_specs = (
        P("spec", "wave"),
        P("spec"),
        P("spec"),
        P("spec"),
        P("spec", None),
        P(None, "wave"),
    )
    out_specs = (P(None, "wave"), P("spec", None))
    return jax.shard_map(
        functools.partial(shards, mesh.shape["spec"], mesh.shape["wave"]),
        mesh=mesh,
        in_specs=in_specs,
        out_specs=out_specs,
        check_vma=False,
    )
```

```python
import functools

import jax
import jax.numpy as jnp
from jax import lax
from jax.experimental import pallas as pl
from jax.experimental.pallas import tpu as pltpu
from jax.sharding import PartitionSpec as P

ITERS = 4
LANES = 128
MESH = pl.DeviceIdType.MESH
F32 = jnp.float32
BF16 = jnp.bfloat16


def shift_kernel(shift_ref, flux_ref, lo_ref, hi_ref, out_ref):
    shift = shift_ref[pl.program_id(0)]
    rows, width = flux_ref.shape
    lane = lax.broadcasted_iota(jnp.int32, (rows, LANES), 1)
    before = jnp.zeros((rows, LANES), F32)
    for tile in range(width // LANES + 1):
        if tile < width // LANES:
            now = flux_ref[:, tile * LANES : (tile + 1) * LANES].astype(F32)
            now = pltpu.roll(now, shift, 1)
        else:
            now = jnp.zeros((rows, LANES), F32)
        moved = jnp.where(lane < shift, before, now)
        column = lane + tile * LANES
        inside = (column >= lo_ref[...]) & (column < hi_ref[...])
        out_ref[:, tile * LANES : (tile + 1) * LANES] = jnp.where(inside, moved, 0.0).astype(BF16)
        before = now


def shifted_rest(spectra, shift, low, high, blocks):
    rows, width = spectra.shape
    per = rows // blocks
    return pl.pallas_call(
        shift_kernel,
        out_shape=jax.ShapeDtypeStruct((rows, width + LANES), BF16),
        grid_spec=pltpu.PrefetchScalarGridSpec(
            num_scalar_prefetch=1,
            grid=(blocks,),
            in_specs=[
                pl.BlockSpec((per, width), lambda i, s: (i, 0)),
                pl.BlockSpec((per, LANES), lambda i, s: (i, 0)),
                pl.BlockSpec((per, LANES), lambda i, s: (i, 0)),
            ],
            out_specs=pl.BlockSpec((per, width + LANES), lambda i, s: (i, 0)),
        ),
        compiler_params=pltpu.CompilerParams(vmem_limit_bytes=32 * 2**20),
    )(shift, spectra, low, high)


def main_kernel(
    n_spec,
    n_wave,
    first_ref,
    rest_ref,
    lo_ref,
    hi_ref,
    coef_ref,
    temp_ref,
    temps_out,
    coef_out,
    wbuf,
    wown,
    wfin,
    hb,
    hown,
    hfin,
    parts,
    send_a,
    recv_a,
    send_b,
    recv_b,
    wide_b,
    recv_wb,
    keep_b,
    send_z,
    recv_z,
    send_c,
    recv_c,
    wide_c,
    recv_wc,
    keep_c,
    den_c,
    den_t,
    s_a,
    r_a,
    s_b,
    r_b,
    s_z,
    r_z,
    s_w,
    r_w,
    s_wb,
    r_wb,
    s_wc,
    r_wc,
    s_c,
    r_c,
    s_h,
    r_h,
    s_f,
    r_f,
    s_g,
    r_g,
):
    spec = lax.axis_index("spec")
    wave = lax.axis_index("wave")
    chips = n_spec // 2
    chip = spec // 2
    core = spec % 2
    buddy = 1 - core
    rows, _ = hb.shape
    blocks = first_ref.shape[0]
    per = rows // blocks
    own = rows // n_wave
    tiles = wbuf.shape[1]
    chunk = tiles // n_wave
    rank_part = wbuf.shape[2]
    rank = n_spec * rank_part
    spans = rest_ref.shape[1] // LANES
    group = max(g for g in range(1, 6) if spans % g == 0)
    some = max(g for g in range(1, 8) if chunk % g == 0)
    unit = min(own, per)
    units = rows // unit
    own_rows = pl.ds(pl.multiple_of(wave * own, own), own)

    def chip_at(k):
        if chips == 4:
            return [chip, chip + 1 - 2 * (chip % 2), lax.rem(chip + 2, 4), 3 - chip][k]
        return lax.rem(chip + k, chips)

    def chip_from(k):
        return chip_at(k) if chips == 4 else lax.rem(chip + chips - k, chips)

    def to_chip(k):
        return (chip_at(k) * 2 + core, wave)

    def to_buddy():
        return (chip * 2 + buddy, wave)

    def to_wave(k):
        return (spec, lax.rem(wave + k, n_wave))

    def to_spec(k):
        return (lax.rem(spec + k, n_spec), wave)

    def copy(src, dst, send, recv, device):
        return pltpu.make_async_remote_copy(
            src_ref=src, dst_ref=dst, send_sem=send, recv_sem=recv, device_id=device, device_id_type=MESH
        )

    def part_of(k):
        return pl.ds(lax.rem(wave + k, n_wave) * chunk, chunk)

    def part_from(k):
        return pl.ds(lax.rem(wave + n_wave - k, n_wave) * chunk, chunk)

    barrier = pltpu.get_barrier_semaphore()
    for k in range(1, n_spec):
        pl.semaphore_signal(barrier, inc=1, device_id=to_spec(k), device_id_type=MESH)
    for k in range(1, n_wave):
        pl.semaphore_signal(barrier, inc=1, device_id=to_wave(k), device_id_type=MESH)
    pl.semaphore_wait(barrier, n_spec + n_wave - 2)

    def gather_templates(arrived=None):
        over_z = [None] + [
            copy(wbuf.at[spec, part_of(0)], wbuf.at[spec, part_of(0)], s_w.at[k], r_w.at[k], to_wave(k))
            for k in range(1, n_wave)
        ]
        over_chips = {}
        over_core = {}
        for kz in range(n_wave):
            for k in range(chips):
                slot = wbuf.at[chip_from(k) * 2 + core, part_from(kz)]
                over_core[kz, k] = copy(slot, slot, s_wc.at[kz, k], r_wc.at[kz, k], to_buddy())
                if chips == 4 and k == 3:
                    slot = wbuf.at[chip_at(1 + kz % 2) * 2 + core, part_from(kz)]
                    over_chips[kz, k] = copy(
                        slot, slot, s_wb.at[kz, k], r_wb.at[kz, k], to_chip(2 - kz % 2)
                    )
                elif k:
                    mine = wbuf.at[spec, part_from(kz)]
                    over_chips[kz, k] = copy(mine, mine, s_wb.at[kz, k], r_wb.at[kz, k], to_chip(k))
        direct = range(1, 3) if chips == 4 else range(1, chips)
        relayed = range(3, 4) if chips == 4 else ()
        for k in range(1, n_wave):
            over_z[k].start()
        for stage in range(n_wave + 3):
            if stage < n_wave:
                if stage:
                    over_z[stage].wait_recv()
                for k in direct:
                    over_chips[stage, k].start()
                over_core[stage, 0].start()
            if 1 <= stage <= n_wave:
                kz = stage - 1
                for k in direct:
                    over_chips[kz, k].wait_recv()
                    for other in relayed:
                        if k == 1 + kz % 2:
                            over_chips[kz, other].start()
                    over_core[kz, k].start()
            if 2 <= stage <= n_wave + 1:
                kz = stage - 2
                for k in relayed:
                    over_chips[kz, k].wait_recv()
                    over_core[kz, k].start()
            if stage >= 3:
                kz = stage - 3
                for k in range(chips):
                    over_core[kz, k].wait_recv()
                if arrived is not None:
                    arrived(kz)
        for kz in range(n_wave):
            for k in range(chips):
                over_core[kz, k].wait_send()
                if k:
                    over_chips[kz, k].wait_send()
            if kz:
                over_z[kz].wait_send()

    def tile_of(index):
        piece = wbuf[:, index]
        if rank_part % 16:
            return piece.astype(F32).reshape(rank, LANES).astype(BF16)
        return piece.reshape(rank, LANES)

    def rows_of(at):
        return pl.ds(pl.multiple_of(at * unit, unit), unit)

    def ratio_of(at, g):
        start = first_ref[at * unit // per] + g * group
        temps = jnp.concatenate(
            [tile_of(jnp.clip(start + k, 0, tiles - 1)) for k in range(group)], axis=1
        )
        model = jnp.dot(hb[rows_of(at), :], temps, preferred_element_type=F32)
        rest = rest_ref[rows_of(at), g * group * LANES : (g + 1) * group * LANES].astype(F32)
        inverse = pl.reciprocal(model, approx=True)
        inverse = inverse * (2.0 - model * inverse)
        return temps, jnp.where(rest > 0, rest * inverse, 0.0).astype(BF16)

    def change_of(value, share, held):
        wanted = value * share
        sent = (wanted - held).astype(BF16)
        held = held + sent.astype(F32)
        left = jnp.where(held > 0, wanted / held, 1.0)
        return sent, held, jnp.clip(left, 0.99, 1.01)

    def put_stat(index, value):
        for part in range(n_spec):
            send_a[part % 2, part // 2, index] = value[part * rank_part : (part + 1) * rank_part]

    def mask_of(low, high, first):
        pixel = lax.broadcasted_iota(jnp.int32, low.shape, 1) + first
        return jnp.where((pixel >= low) & (pixel < high), 1.0, 0.0).astype(BF16)

    def coef_copies():
        return [
            copy(hb.at[own_rows], hb.at[own_rows], s_h.at[k], r_h.at[k], to_wave(k))
            for k in range(1, n_wave)
        ]

    wown[...] = temp_ref[...]
    wbuf[spec, part_of(0)] = temp_ref[...].astype(BF16)
    hb[own_rows, :] = coef_ref[own_rows, :].astype(BF16)
    hown[...] = coef_ref[own_rows, :]
    for one in coef_copies():
        one.start()
    for at in range(units):
        parts[at, 0] = jnp.zeros((rank, LANES), F32)
        parts[at, spans + 1] = jnp.zeros((rank, LANES), F32)
    keep_b[...] = jnp.ones_like(keep_b)
    keep_c[...] = jnp.ones_like(keep_c)
    gather_templates()

    last_temps = [
        copy(wown, wfin.at[spec], s_f.at[k], r_f.at[k], to_spec(k)) for k in range(1, n_spec)
    ]
    order = list(range(1, n_wave)) + [0]

    def update(opening, step):
        out_b, in_b = (wide_b, recv_wb) if opening else (send_b, recv_b)
        out_c, in_c = (wide_c, recv_wc) if opening else (send_c, recv_c)

        copies_a = {}
        copies_b = {}
        for kz in range(n_wave + 1):
            where = part_of(kz) if kz < n_wave else pl.ds(tiles, chunk)
            copies_a[kz] = copy(
                send_a.at[buddy, :, where], recv_a.at[:, where], s_a.at[kz], r_a.at[kz], to_buddy()
            )
            for k in range(1, chips):
                source, target = (out_b, in_b) if kz < n_wave else (wide_b, recv_wb)
                copies_b[kz, k] = copy(
                    source.at[k - 1, where], target.at[k - 1, where], s_b.at[kz, k], r_b.at[kz, k], to_chip(k)
                )
        copies_z = {
            k: copy(send_z.at[k - 1], recv_z.at[k - 1], s_z.at[k], r_z.at[k], to_wave(k))
            for k in range(1, n_wave)
        }

        def send_sums(kz):
            first = lax.rem(wave + kz, n_wave) * chunk if kz < n_wave else tiles
            copies_a[kz].wait_recv()

            def add_core(i, unused):
                index = first + i
                for k in range(1, chips):
                    c = chip_at(k)
                    value = send_a[core, c, index] + recv_a[c, index]
                    if kz == n_wave or opening:
                        wide_b[k - 1, index] = value
                    else:
                        send_b[k - 1, index], wide_b[k - 1, index], keep_b[k - 1, index] = change_of(
                            value, keep_b[k - 1, index], wide_b[k - 1, index]
                        )
                return 0

            lax.fori_loop(0, chunk, add_core, 0)
            for k in range(1, chips):
                copies_b[kz, k].start()

        copies_h = coef_copies()
        for kz in range(n_wave):
            if kz:
                copies_h[kz - 1].wait()
            for j in range(own // unit):
                at = lax.rem(wave + n_wave - kz, n_wave) * (own // unit) + j

                def some_dens(i, unused):
                    index = i * some
                    masks = [
                        mask_of(
                            lo_ref[rows_of(at), :],
                            hi_ref[rows_of(at), :],
                            (wave * chunk + index + k) * LANES,
                        )
                        for k in range(some)
                    ]
                    den = lax.dot_general(
                        hb[rows_of(at), :],
                        jnp.concatenate(masks, axis=1),
                        (((0,), (0,)), ((), ())),
                        preferred_element_type=F32,
                    )
                    for k in range(some):
                        piece = den[:, k * LANES : (k + 1) * LANES]
                        if kz == 0 and j == 0:
                            den_t[index + k] = piece
                        else:
                            den_t[index + k] += piece
                    return 0

                lax.fori_loop(0, chunk // some, some_dens, 0)
                if kz == n_wave - 1 and j == own // unit - 1:

                    def put_den(i, unused):
                        put_stat(tiles + i, den_t[i])
                        return 0

                    lax.fori_loop(0, chunk, put_den, 0)
                    copies_a[n_wave].start()
                for g in range(spans // group):
                    temps, ratio = ratio_of(at, g)
                    num = lax.dot_general(
                        hb[rows_of(at), :], ratio, (((0,), (0,)), ((), ())), preferred_element_type=F32
                    )
                    for k in range(group):
                        parts[at, 1 + g * group + k] = num[:, k * LANES : (k + 1) * LANES]
        send_sums(n_wave)

        for kz in order:
            first = lax.rem(wave + kz, n_wave) * chunk

            def add_blocks(i, unused):
                index = first + i
                total = None
                for at in range(units):
                    place = jnp.clip(index - first_ref[at * unit // per], -1, spans) + 1
                    total = parts[at, place] if at == 0 else total + parts[at, place]
                put_stat(index, total)
                return 0

            lax.fori_loop(0, chunk, add_blocks, 0)
            copies_a[kz].start()

        for kz in order:
            send_sums(kz)

        def chip_sum(index, den=False):
            total = send_a[core, chip, index] + recv_a[chip, index]
            for k in range(1, chips):
                landed = recv_wb[k - 1, index]
                if not (opening or den):
                    landed = landed + recv_b[k - 1, index].astype(F32)
                    recv_wb[k - 1, index] = landed
                total = total + landed
            return total

        for kz in order[:-1]:
            first = lax.rem(wave + kz, n_wave) * chunk
            for k in range(1, chips):
                copies_b[kz, k].wait_recv()

            def add_chips(i, unused):
                send_z[kz - 1, i] = chip_sum(first + i)
                return 0

            lax.fori_loop(0, chunk, add_chips, 0)
            copies_z[kz].start()
        for kz in (0, n_wave):
            for k in range(1, chips):
                copies_b[kz, k].wait_recv()
        for k in range(1, n_wave):
            copies_z[k].wait_recv()

        def new_tile(i, unused):
            num = chip_sum(wave * chunk + i)
            for k in range(1, n_wave):
                num = num + recv_z[k - 1, i]
            value = wown[i] * num / jnp.maximum(chip_sum(tiles + i, True), 1.0)
            wown[i] = value
            wbuf[spec, wave * chunk + i] = value.astype(BF16)
            return 0

        lax.fori_loop(0, chunk, new_tile, 0)
        for kz in range(n_wave + 1):
            copies_a[kz].wait_send()
            for k in range(1, chips):
                copies_b[kz, k].wait_send()
        for k in range(1, n_wave):
            copies_z[k].wait_send()

        den_c[...] = jnp.zeros_like(den_c)

        def add_den(kz):
            first = lax.rem(wave + n_wave - kz, n_wave) * chunk

            def some_tiles(i, unused):
                index = first + i * some
                masks = [
                    mask_of(lo_ref[own_rows, :], hi_ref[own_rows, :], (index + k) * LANES)
                    for k in range(some)
                ]
                den_c[...] += lax.dot_general(
                    jnp.concatenate(masks, axis=1),
                    jnp.concatenate([tile_of(index + k) for k in range(some)], axis=1),
                    (((1,), (1,)), ((), ())),
                    preferred_element_type=F32,
                )
                return 0

            lax.fori_loop(0, chunk // some, some_tiles, 0)

        gather_templates(add_den)

        if not opening:

            @pl.when(step == ITERS - 1)
            def _():
                for one in last_temps:
                    one.start()

        copies_c = [
            copy(out_c.at[k - 1], in_c.at[k - 1], s_c.at[k], r_c.at[k], to_wave(k))
            for k in range(1, n_wave)
        ]
        mine = None
        for kz in order:
            pieces = []
            for j in range(own // unit):
                at = lax.rem(wave + kz, n_wave) * (own // unit) + j
                total = None
                for g in range(spans // group):
                    temps, ratio = ratio_of(at, g)
                    num = lax.dot_general(
                        ratio, temps, (((1,), (1,)), ((), ())), preferred_element_type=F32
                    )
                    total = num if g == 0 else total + num
                pieces.append(total)
            total = pieces[0] if len(pieces) == 1 else jnp.concatenate(pieces, axis=0)
            if kz == 0:
                mine = total
            else:
                if opening:
                    wide_c[kz - 1] = total
                else:
                    send_c[kz - 1], wide_c[kz - 1], keep_c[kz - 1] = change_of(
                        total, keep_c[kz - 1], wide_c[kz - 1]
                    )
                copies_c[kz - 1].start()
        for one in copies_c:
            one.wait_recv()
        for k in range(1, n_wave):
            landed = recv_wc[k - 1]
            if not opening:
                landed = landed + recv_c[k - 1].astype(F32)
                recv_wc[k - 1] = landed
            mine = mine + landed
        value = hown[...] * mine / jnp.maximum(den_c[...], 1.0)
        hown[...] = value
        for one in copies_c:
            one.wait_send()

        @pl.when(step < ITERS - 1)
        def _():
            hb[own_rows, :] = value.astype(BF16)
            for one in coef_copies():
                one.start()

    def later(step, unused):
        update(False, step)
        return 0

    update(True, 0)
    lax.fori_loop(1, ITERS, later, 0)

    last_coefs = [
        copy(hown, hfin.at[wave], s_g.at[k], r_g.at[k], to_wave(k)) for k in range(1, n_wave)
    ]
    for one in last_coefs:
        one.start()
    wfin[spec] = wown[...]
    hfin[wave] = hown[...]
    for one in last_temps:
        one.wait()
    for i in range(chunk):
        temps_out[:, i * LANES : (i + 1) * LANES] = wfin[:, i].reshape(rank, LANES)
    for one in last_coefs:
        one.wait()
    for k in range(n_wave):
        coef_out[k * own : (k + 1) * own, :] = hfin[k]


def shards(n_spec, n_wave, spectra, offsets, cover_lo, cover_hi, coefficients, templates):
    rows, width = spectra.shape
    rank = templates.shape[0]
    blocks = offsets.shape[0]
    chips = n_spec // 2
    chunk = width // LANES
    tiles = chunk * n_wave
    part = rank // n_spec
    own = rows // n_wave
    wave = lax.axis_index("wave")
    spec = lax.axis_index("spec")

    base = wave * width - offsets
    shift = jnp.mod(base, LANES)
    first = (base - shift) // LANES
    row_off, row_shift = (jnp.repeat(v, rows // blocks) for v in (offsets, shift))
    begin = wave * width
    low = jnp.maximum(jnp.maximum(cover_lo - begin, 0), row_off - begin) + row_shift
    high = jnp.minimum(cover_hi - begin, width) + row_shift

    def spread(value):
        return jnp.broadcast_to(value[:, None], (rows, LANES))

    rest = shifted_rest(spectra, shift, spread(low), spread(high), blocks)
    mine = lax.dynamic_slice_in_dim(templates, spec * part, part, 0)
    mine = mine.reshape(part, chunk, LANES).transpose(1, 0, 2)

    vmem = pl.BlockSpec(memory_space=pltpu.VMEM)
    dma = pltpu.SemaphoreType.DMA
    return pl.pallas_call(
        functools.partial(main_kernel, n_spec, n_wave),
        out_shape=(
            jax.ShapeDtypeStruct((rank, width), F32),
            jax.ShapeDtypeStruct((rows, rank), F32),
        ),
        in_specs=[pl.BlockSpec(memory_space=pltpu.SMEM)] + [vmem] * 5,
        out_specs=(vmem, vmem),
        scratch_shapes=[
            pltpu.VMEM((n_spec, tiles, part, LANES), BF16),
            pltpu.VMEM((chunk, part, LANES), F32),
            pltpu.VMEM((n_spec, chunk, part, LANES), F32),
            pltpu.VMEM((rows, rank), BF16),
            pltpu.VMEM((own, rank), F32),
            pltpu.VMEM((n_wave, own, rank), F32),
            pltpu.VMEM((rows // min(own, rows // blocks), chunk + 3, rank, LANES), F32),
            pltpu.VMEM((2, chips, tiles + chunk, part, LANES), F32),
            pltpu.VMEM((chips, tiles + chunk, part, LANES), F32),
            pltpu.VMEM((chips - 1, tiles + chunk, part, LANES), BF16),
            pltpu.VMEM((chips - 1, tiles + chunk, part, LANES), BF16),
            pltpu.VMEM((chips - 1, tiles + chunk, part, LANES), F32),
            pltpu.VMEM((chips - 1, tiles + chunk, part, LANES), F32),
            pltpu.VMEM((chips - 1, tiles + chunk, part, LANES), F32),
            pltpu.VMEM((n_wave - 1, chunk, part, LANES), F32),
            pltpu.VMEM((n_wave - 1, chunk, part, LANES), F32),
            pltpu.VMEM((n_wave - 1, own, rank), BF16),
            pltpu.VMEM((n_wave - 1, own, rank), BF16),
            pltpu.VMEM((n_wave - 1, own, rank), F32),
            pltpu.VMEM((n_wave - 1, own, rank), F32),
            pltpu.VMEM((n_wave - 1, own, rank), F32),
            pltpu.VMEM((own, rank), F32),
            pltpu.VMEM((chunk, rank, LANES), F32),
        ]
        + [dma((n_wave + 1,))] * 2
        + [dma((n_wave + 1, chips))] * 2
        + [dma((n_wave,))] * 2
        + [dma((n_wave,))] * 2
        + [dma((n_wave, chips))] * 4
        + [dma((n_wave,))] * 2
        + [dma((n_wave,))] * 2
        + [dma((n_spec,))] * 2
        + [dma((n_wave,))] * 2,
        compiler_params=pltpu.CompilerParams(
            collective_id=0, has_side_effects=True, vmem_limit_bytes=48 * 2**20
        ),
    )(
        first,
        rest,
        spread(cover_lo - row_off),
        spread(cover_hi - row_off),
        coefficients,
        mine,
    )


def solution(mesh):
    in_specs = (
        P("spec", "wave"),
        P("spec"),
        P("spec"),
        P("spec"),
        P("spec", None),
        P(None, "wave"),
    )
    out_specs = (P(None, "wave"), P("spec", None))
    return jax.shard_map(
        functools.partial(shards, mesh.shape["spec"], mesh.shape["wave"]),
        mesh=mesh,
        in_specs=in_specs,
        out_specs=out_specs,
        check_vma=False,
    )
```

```python
import functools

import jax
import jax.numpy as jnp
from jax import lax
from jax.experimental import pallas as pl
from jax.experimental.pallas import tpu as pltpu
from jax.sharding import PartitionSpec as P

ITERS = 4
LANES = 128
MESH = pl.DeviceIdType.MESH
F32 = jnp.float32
BF16 = jnp.bfloat16


def shift_kernel(shift_ref, flux_ref, lo_ref, hi_ref, out_ref):
    shift = shift_ref[pl.program_id(0)]
    rows, width = flux_ref.shape
    lane = lax.broadcasted_iota(jnp.int32, (rows, LANES), 1)
    before = jnp.zeros((rows, LANES), F32)
    for tile in range(width // LANES + 1):
        if tile < width // LANES:
            now = flux_ref[:, tile * LANES : (tile + 1) * LANES].astype(F32)
            now = pltpu.roll(now, shift, 1)
        else:
            now = jnp.zeros((rows, LANES), F32)
        moved = jnp.where(lane < shift, before, now)
        column = lane + tile * LANES
        inside = (column >= lo_ref[...]) & (column < hi_ref[...])
        out_ref[:, tile * LANES : (tile + 1) * LANES] = jnp.where(inside, moved, 0.0).astype(BF16)
        before = now


def shifted_rest(spectra, shift, low, high, blocks):
    rows, width = spectra.shape
    per = rows // blocks
    return pl.pallas_call(
        shift_kernel,
        out_shape=jax.ShapeDtypeStruct((rows, width + LANES), BF16),
        grid_spec=pltpu.PrefetchScalarGridSpec(
            num_scalar_prefetch=1,
            grid=(blocks,),
            in_specs=[
                pl.BlockSpec((per, width), lambda i, s: (i, 0)),
                pl.BlockSpec((per, LANES), lambda i, s: (i, 0)),
                pl.BlockSpec((per, LANES), lambda i, s: (i, 0)),
            ],
            out_specs=pl.BlockSpec((per, width + LANES), lambda i, s: (i, 0)),
        ),
        compiler_params=pltpu.CompilerParams(vmem_limit_bytes=32 * 2**20),
    )(shift, spectra, low, high)


def main_kernel(
    n_spec,
    n_wave,
    first_ref,
    rest_ref,
    lo_ref,
    hi_ref,
    coef_ref,
    temp_ref,
    temps_out,
    coef_out,
    wbuf,
    wown,
    wfin,
    hb,
    hown,
    hfin,
    parts,
    send_a,
    recv_a,
    send_b,
    recv_b,
    wide_b,
    recv_wb,
    keep_b,
    send_z,
    recv_z,
    send_c,
    recv_c,
    wide_c,
    recv_wc,
    keep_c,
    den_c,
    s_a,
    r_a,
    s_b,
    r_b,
    s_z,
    r_z,
    s_w,
    r_w,
    s_wb,
    r_wb,
    s_wc,
    r_wc,
    s_c,
    r_c,
    s_h,
    r_h,
    s_f,
    r_f,
    s_g,
    r_g,
):
    spec = lax.axis_index("spec")
    wave = lax.axis_index("wave")
    chips = n_spec // 2
    chip = spec // 2
    core = spec % 2
    buddy = 1 - core
    rows, _ = hb.shape
    blocks = first_ref.shape[0]
    per = rows // blocks
    own = rows // n_wave
    tiles = wbuf.shape[1]
    chunk = tiles // n_wave
    rank_part = wbuf.shape[2]
    rank = n_spec * rank_part
    spans = rest_ref.shape[1] // LANES
    group = max(g for g in range(1, 6) if spans % g == 0)
    some = max(g for g in range(1, 8) if chunk % g == 0)
    unit = min(own, per)
    units = rows // unit
    own_rows = pl.ds(pl.multiple_of(wave * own, own), own)

    def to_chip(k):
        return (lax.rem(chip + k, chips) * 2 + core, wave)

    def to_buddy():
        return (chip * 2 + buddy, wave)

    def to_wave(k):
        return (spec, lax.rem(wave + k, n_wave))

    def to_spec(k):
        return (lax.rem(spec + k, n_spec), wave)

    def copy(src, dst, send, recv, device):
        return pltpu.make_async_remote_copy(
            src_ref=src, dst_ref=dst, send_sem=send, recv_sem=recv, device_id=device, device_id_type=MESH
        )

    def part_of(k):
        return pl.ds(lax.rem(wave + k, n_wave) * chunk, chunk)

    def part_from(k):
        return pl.ds(lax.rem(wave + n_wave - k, n_wave) * chunk, chunk)

    barrier = pltpu.get_barrier_semaphore()
    for k in range(1, n_spec):
        pl.semaphore_signal(barrier, inc=1, device_id=to_spec(k), device_id_type=MESH)
    for k in range(1, n_wave):
        pl.semaphore_signal(barrier, inc=1, device_id=to_wave(k), device_id_type=MESH)
    pl.semaphore_wait(barrier, n_spec + n_wave - 2)

    def gather_templates(arrived=None):
        over_z = [None] + [
            copy(wbuf.at[spec, part_of(0)], wbuf.at[spec, part_of(0)], s_w.at[k], r_w.at[k], to_wave(k))
            for k in range(1, n_wave)
        ]
        over_chips = {}
        over_core = {}
        for kz in range(n_wave):
            for k in range(chips):
                slot = wbuf.at[lax.rem(chip + chips - k, chips) * 2 + core, part_from(kz)]
                over_core[kz, k] = copy(slot, slot, s_wc.at[kz, k], r_wc.at[kz, k], to_buddy())
                if k:
                    mine = wbuf.at[spec, part_from(kz)]
                    over_chips[kz, k] = copy(mine, mine, s_wb.at[kz, k], r_wb.at[kz, k], to_chip(k))
        for k in range(1, n_wave):
            over_z[k].start()
        for kz in range(n_wave):
            if kz:
                over_z[kz].wait_recv()
            for k in range(1, chips):
                over_chips[kz, k].start()
            over_core[kz, 0].start()
        for kz in range(n_wave + 1):
            if kz < n_wave:
                for k in range(1, chips):
                    over_chips[kz, k].wait_recv()
                    over_core[kz, k].start()
            if kz:
                for k in range(chips):
                    over_core[kz - 1, k].wait_recv()
                if arrived is not None:
                    arrived(kz - 1)
        for kz in range(n_wave):
            for k in range(chips):
                over_core[kz, k].wait_send()
                if k:
                    over_chips[kz, k].wait_send()
            if kz:
                over_z[kz].wait_send()

    def tile_of(index):
        piece = wbuf[:, index]
        if rank_part % 16:
            return piece.astype(F32).reshape(rank, LANES).astype(BF16)
        return piece.reshape(rank, LANES)

    def rows_of(at):
        return pl.ds(pl.multiple_of(at * unit, unit), unit)

    def ratio_of(at, g):
        start = first_ref[at * unit // per] + g * group
        temps = jnp.concatenate(
            [tile_of(jnp.clip(start + k, 0, tiles - 1)) for k in range(group)], axis=1
        )
        model = jnp.dot(hb[rows_of(at), :], temps, preferred_element_type=F32)
        rest = rest_ref[rows_of(at), g * group * LANES : (g + 1) * group * LANES].astype(F32)
        return temps, jnp.where(rest > 0, rest / model, 0.0).astype(BF16)

    def change_of(value, share, held):
        wanted = value * share
        sent = (wanted - held).astype(BF16)
        held = held + sent.astype(F32)
        left = jnp.where(held > 0, wanted / held, 1.0)
        return sent, held, jnp.clip(left, 0.99, 1.01)

    def put_stat(index, value):
        for part in range(n_spec):
            send_a[part % 2, part // 2, index] = value[part * rank_part : (part + 1) * rank_part]

    def mask_of(low, high, first):
        pixel = lax.broadcasted_iota(jnp.int32, low.shape, 1) + first
        return jnp.where((pixel >= low) & (pixel < high), 1.0, 0.0).astype(BF16)

    def coef_copies():
        return [
            copy(hb.at[own_rows], hb.at[own_rows], s_h.at[k], r_h.at[k], to_wave(k))
            for k in range(1, n_wave)
        ]

    wown[...] = temp_ref[...]
    wbuf[spec, part_of(0)] = temp_ref[...].astype(BF16)
    hb[own_rows, :] = coef_ref[own_rows, :].astype(BF16)
    hown[...] = coef_ref[own_rows, :]
    for one in coef_copies():
        one.start()
    for at in range(units):
        parts[at, 0] = jnp.zeros((rank, LANES), F32)
        parts[at, spans + 1] = jnp.zeros((rank, LANES), F32)
    keep_b[...] = jnp.ones_like(keep_b)
    keep_c[...] = jnp.ones_like(keep_c)
    gather_templates()

    last_temps = [
        copy(wown, wfin.at[spec], s_f.at[k], r_f.at[k], to_spec(k)) for k in range(1, n_spec)
    ]
    order = list(range(1, n_wave)) + [0]

    def update(opening, step):
        out_b, in_b = (wide_b, recv_wb) if opening else (send_b, recv_b)
        out_c, in_c = (wide_c, recv_wc) if opening else (send_c, recv_c)

        copies_h = coef_copies()
        for kz in range(n_wave):
            if kz:
                copies_h[kz - 1].wait()
            for j in range(own // unit):
                at = lax.rem(wave + n_wave - kz, n_wave) * (own // unit) + j
                for g in range(spans // group):
                    temps, ratio = ratio_of(at, g)
                    num = lax.dot_general(
                        hb[rows_of(at), :], ratio, (((0,), (0,)), ((), ())), preferred_element_type=F32
                    )
                    for k in range(group):
                        parts[at, 1 + g * group + k] = num[:, k * LANES : (k + 1) * LANES]

        copies_a = {}
        copies_b = {}
        for kz in range(n_wave + 1):
            where = part_of(kz) if kz < n_wave else pl.ds(tiles, chunk)
            copies_a[kz] = copy(
                send_a.at[buddy, :, where], recv_a.at[:, where], s_a.at[kz], r_a.at[kz], to_buddy()
            )
            for k in range(1, chips):
                source, target = (out_b, in_b) if kz < n_wave else (wide_b, recv_wb)
                copies_b[kz, k] = copy(
                    source.at[k - 1, where], target.at[k - 1, where], s_b.at[kz, k], r_b.at[kz, k], to_chip(k)
                )
        copies_z = {
            k: copy(send_z.at[k - 1], recv_z.at[k - 1], s_z.at[k], r_z.at[k], to_wave(k))
            for k in range(1, n_wave)
        }

        for kz in order:
            first = lax.rem(wave + kz, n_wave) * chunk

            def add_blocks(i, unused):
                index = first + i
                total = None
                for at in range(units):
                    place = jnp.clip(index - first_ref[at * unit // per], -1, spans) + 1
                    total = parts[at, place] if at == 0 else total + parts[at, place]
                put_stat(index, total)
                return 0

            lax.fori_loop(0, chunk, add_blocks, 0)
            copies_a[kz].start()

        def den_tile(i, unused):
            mask = mask_of(lo_ref[...], hi_ref[...], (wave * chunk + i) * LANES)
            put_stat(
                tiles + i,
                lax.dot_general(hb[...], mask, (((0,), (0,)), ((), ())), preferred_element_type=F32),
            )
            return 0

        lax.fori_loop(0, chunk, den_tile, 0)
        copies_a[n_wave].start()

        for kz in order + [n_wave]:
            first = lax.rem(wave + kz, n_wave) * chunk if kz < n_wave else tiles
            copies_a[kz].wait_recv()

            def add_core(i, unused):
                index = first + i
                for k in range(1, chips):
                    c = lax.rem(chip + k, chips)
                    value = send_a[core, c, index] + recv_a[c, index]
                    if kz == n_wave or opening:
                        wide_b[k - 1, index] = value
                    else:
                        send_b[k - 1, index], wide_b[k - 1, index], keep_b[k - 1, index] = change_of(
                            value, keep_b[k - 1, index], wide_b[k - 1, index]
                        )
                return 0

            lax.fori_loop(0, chunk, add_core, 0)
            for k in range(1, chips):
                copies_b[kz, k].start()

        def chip_sum(index, den=False):
            total = send_a[core, chip, index] + recv_a[chip, index]
            for k in range(1, chips):
                landed = recv_wb[k - 1, index]
                if not (opening or den):
                    landed = landed + recv_b[k - 1, index].astype(F32)
                    recv_wb[k - 1, index] = landed
                total = total + landed
            return total

        for kz in order[:-1]:
            first = lax.rem(wave + kz, n_wave) * chunk
            for k in range(1, chips):
                copies_b[kz, k].wait_recv()

            def add_chips(i, unused):
                send_z[kz - 1, i] = chip_sum(first + i)
                return 0

            lax.fori_loop(0, chunk, add_chips, 0)
            copies_z[kz].start()
        for kz in (0, n_wave):
            for k in range(1, chips):
                copies_b[kz, k].wait_recv()
        for k in range(1, n_wave):
            copies_z[k].wait_recv()

        def new_tile(i, unused):
            num = chip_sum(wave * chunk + i)
            for k in range(1, n_wave):
                num = num + recv_z[k - 1, i]
            value = wown[i] * num / jnp.maximum(chip_sum(tiles + i, True), 1.0)
            wown[i] = value
            wbuf[spec, wave * chunk + i] = value.astype(BF16)
            return 0

        lax.fori_loop(0, chunk, new_tile, 0)
        for kz in range(n_wave + 1):
            copies_a[kz].wait_send()
            for k in range(1, chips):
                copies_b[kz, k].wait_send()
        for k in range(1, n_wave):
            copies_z[k].wait_send()

        den_c[...] = jnp.zeros_like(den_c)

        def add_den(kz):
            first = lax.rem(wave + n_wave - kz, n_wave) * chunk

            def some_tiles(i, unused):
                index = first + i * some
                masks = [
                    mask_of(lo_ref[own_rows, :], hi_ref[own_rows, :], (index + k) * LANES)
                    for k in range(some)
                ]
                den_c[...] += lax.dot_general(
                    jnp.concatenate(masks, axis=1),
                    jnp.concatenate([tile_of(index + k) for k in range(some)], axis=1),
                    (((1,), (1,)), ((), ())),
                    preferred_element_type=F32,
                )
                return 0

            lax.fori_loop(0, chunk // some, some_tiles, 0)

        gather_templates(add_den)

        if not opening:

            @pl.when(step == ITERS - 1)
            def _():
                for one in last_temps:
                    one.start()

        copies_c = [
            copy(out_c.at[k - 1], in_c.at[k - 1], s_c.at[k], r_c.at[k], to_wave(k))
            for k in range(1, n_wave)
        ]
        mine = None
        for kz in order:
            pieces = []
            for j in range(own // unit):
                at = lax.rem(wave + kz, n_wave) * (own // unit) + j
                total = None
                for g in range(spans // group):
                    temps, ratio = ratio_of(at, g)
                    num = lax.dot_general(
                        ratio, temps, (((1,), (1,)), ((), ())), preferred_element_type=F32
                    )
                    total = num if g == 0 else total + num
                pieces.append(total)
            total = pieces[0] if len(pieces) == 1 else jnp.concatenate(pieces, axis=0)
            if kz == 0:
                mine = total
            else:
                if opening:
                    wide_c[kz - 1] = total
                else:
                    send_c[kz - 1], wide_c[kz - 1], keep_c[kz - 1] = change_of(
                        total, keep_c[kz - 1], wide_c[kz - 1]
                    )
                copies_c[kz - 1].start()
        for one in copies_c:
            one.wait_recv()
        for k in range(1, n_wave):
            landed = recv_wc[k - 1]
            if not opening:
                landed = landed + recv_c[k - 1].astype(F32)
                recv_wc[k - 1] = landed
            mine = mine + landed
        value = hown[...] * mine / jnp.maximum(den_c[...], 1.0)
        hown[...] = value
        for one in copies_c:
            one.wait_send()

        @pl.when(step < ITERS - 1)
        def _():
            hb[own_rows, :] = value.astype(BF16)
            for one in coef_copies():
                one.start()

    def later(step, unused):
        update(False, step)
        return 0

    update(True, 0)
    lax.fori_loop(1, ITERS, later, 0)

    last_coefs = [
        copy(hown, hfin.at[wave], s_g.at[k], r_g.at[k], to_wave(k)) for k in range(1, n_wave)
    ]
    for one in last_coefs:
        one.start()
    wfin[spec] = wown[...]
    hfin[wave] = hown[...]
    for one in last_temps:
        one.wait()
    for i in range(chunk):
        temps_out[:, i * LANES : (i + 1) * LANES] = wfin[:, i].reshape(rank, LANES)
    for one in last_coefs:
        one.wait()
    for k in range(n_wave):
        coef_out[k * own : (k + 1) * own, :] = hfin[k]


def shards(n_spec, n_wave, spectra, offsets, cover_lo, cover_hi, coefficients, templates):
    rows, width = spectra.shape
    rank = templates.shape[0]
    blocks = offsets.shape[0]
    chips = n_spec // 2
    chunk = width // LANES
    tiles = chunk * n_wave
    part = rank // n_spec
    own = rows // n_wave
    wave = lax.axis_index("wave")
    spec = lax.axis_index("spec")

    base = wave * width - offsets
    shift = jnp.mod(base, LANES)
    first = (base - shift) // LANES
    row_off, row_shift = (jnp.repeat(v, rows // blocks) for v in (offsets, shift))
    begin = wave * width
    low = jnp.maximum(jnp.maximum(cover_lo - begin, 0), row_off - begin) + row_shift
    high = jnp.minimum(cover_hi - begin, width) + row_shift

    def spread(value):
        return jnp.broadcast_to(value[:, None], (rows, LANES))

    rest = shifted_rest(spectra, shift, spread(low), spread(high), blocks)
    mine = lax.dynamic_slice_in_dim(templates, spec * part, part, 0)
    mine = mine.reshape(part, chunk, LANES).transpose(1, 0, 2)

    vmem = pl.BlockSpec(memory_space=pltpu.VMEM)
    dma = pltpu.SemaphoreType.DMA
    return pl.pallas_call(
        functools.partial(main_kernel, n_spec, n_wave),
        out_shape=(
            jax.ShapeDtypeStruct((rank, width), F32),
            jax.ShapeDtypeStruct((rows, rank), F32),
        ),
        in_specs=[pl.BlockSpec(memory_space=pltpu.SMEM)] + [vmem] * 5,
        out_specs=(vmem, vmem),
        scratch_shapes=[
            pltpu.VMEM((n_spec, tiles, part, LANES), BF16),
            pltpu.VMEM((chunk, part, LANES), F32),
            pltpu.VMEM((n_spec, chunk, part, LANES), F32),
            pltpu.VMEM((rows, rank), BF16),
            pltpu.VMEM((own, rank), F32),
            pltpu.VMEM((n_wave, own, rank), F32),
            pltpu.VMEM((rows // min(own, rows // blocks), chunk + 3, rank, LANES), F32),
            pltpu.VMEM((2, chips, tiles + chunk, part, LANES), F32),
            pltpu.VMEM((chips, tiles + chunk, part, LANES), F32),
            pltpu.VMEM((chips - 1, tiles + chunk, part, LANES), BF16),
            pltpu.VMEM((chips - 1, tiles + chunk, part, LANES), BF16),
            pltpu.VMEM((chips - 1, tiles + chunk, part, LANES), F32),
            pltpu.VMEM((chips - 1, tiles + chunk, part, LANES), F32),
            pltpu.VMEM((chips - 1, tiles + chunk, part, LANES), F32),
            pltpu.VMEM((n_wave - 1, chunk, part, LANES), F32),
            pltpu.VMEM((n_wave - 1, chunk, part, LANES), F32),
            pltpu.VMEM((n_wave - 1, own, rank), BF16),
            pltpu.VMEM((n_wave - 1, own, rank), BF16),
            pltpu.VMEM((n_wave - 1, own, rank), F32),
            pltpu.VMEM((n_wave - 1, own, rank), F32),
            pltpu.VMEM((n_wave - 1, own, rank), F32),
            pltpu.VMEM((own, rank), F32),
        ]
        + [dma((n_wave + 1,))] * 2
        + [dma((n_wave + 1, chips))] * 2
        + [dma((n_wave,))] * 2
        + [dma((n_wave,))] * 2
        + [dma((n_wave, chips))] * 4
        + [dma((n_wave,))] * 2
        + [dma((n_wave,))] * 2
        + [dma((n_spec,))] * 2
        + [dma((n_wave,))] * 2,
        compiler_params=pltpu.CompilerParams(
            collective_id=0, has_side_effects=True, vmem_limit_bytes=48 * 2**20
        ),
    )(
        first,
        rest,
        spread(cover_lo - row_off),
        spread(cover_hi - row_off),
        coefficients,
        mine,
    )


def solution(mesh):
    in_specs = (
        P("spec", "wave"),
        P("spec"),
        P("spec"),
        P("spec"),
        P("spec", None),
        P(None, "wave"),
    )
    out_specs = (P(None, "wave"), P("spec", None))
    return jax.shard_map(
        functools.partial(shards, mesh.shape["spec"], mesh.shape["wave"]),
        mesh=mesh,
        in_specs=in_specs,
        out_specs=out_specs,
        check_vma=False,
    )
```
